32 devices in a mesh: groups: 2 (over x), expert: 16 (over z, y, core).
Axes of the slice: x: 2, y: 2, z: 4, core: 2. Of those that a mesh axis runs over, the one named last changes fastest.
Arguments:
- act: bfloat16 [4096, 7168], P(('groups', 'expert')), parts along dimension 0, may hold values from -6 to 6
- act_scale: bfloat16 [4096], P(('groups', 'expert')), parts along dimension 0, may hold values from 0.29882812 to 3
- route_ids: int32 [4096, 2], P(('groups', 'expert')), parts along dimension 0, may hold values from 0 to 7, all different within a row; in each aligned block of 128 rows (0 to 127, 128 to 255, ...) at most 64 rows name the same one
- route_weights: float32 [4096, 2], P(('groups', 'expert')), parts along dimension 0, may hold values from 0.2 to 1
- w_gate: bfloat16 [16, 7168, 512], P('expert'), may hold values from -127 to 127
- w_up: bfloat16 [16, 7168, 512], P('expert'), may hold values from -127 to 127
- w_down: bfloat16 [16, 512, 7168], P('expert'), may hold values from -127 to 127
- gate_scale: float32 [16, 512], P('expert'), may hold values from 8e-05 to 0.00032
- up_scale: float32 [16, 512], P('expert'), may hold values from 8e-05 to 0.00032
- down_scale: float32 [8, 7168], replicated, may hold values from 0.0004 to 0.0016
Outputs:
- mixed: bfloat16 [4096, 7168], P(('groups', 'expert')), parts along dimension 0
The draws below stay inside these ranges and needn't reach their ends.
There are 2 independent parts, one for each index of `groups`. The reference program is written for one: setup_inputs(seed, part) draws one part's arguments, and reference() takes and returns one part's arrays. A program takes and returns all parts, laid end to end along the dimension named above; an argument that names none is the same for every part. Nothing has to cross between parts.
Inputs may be any that keep to these rules, and one draw needn't show every extreme that they name: `route_ids`: each row names 2 different experts; among the rows of one device no expert is named by more than 64 rows, a bound that some block reaches.
All inputs are finite; a program needn't handle non-finite values.
Results may differ from the reference program's by a relative error of at most 0.0066.
Values may be sent and summed in bfloat16 or wider, within the bound.
A program may use at most 128 MiB of HBM per device.

```python
import math
import jax
import jax.numpy as jnp
import numpy as np
from jax import lax

D = 7168
PIECES = 2
TOP = 2
TOK_DEV = 128
HID = 512
EXPERTS = 8
CAP = 64
TOKENS = 2048
N_EXPERT = 16


def integer_table(key, salt, shape):
    mixed = jax.random.fold_in(key, salt)
    return jax.random.randint(mixed, shape, -127, 128).astype(jnp.float32).astype(jnp.bfloat16)


def draw_w_gate(key, part):
    return integer_table(key, 101, (EXPERTS * PIECES, D, HID))


def draw_w_up(key, part):
    return integer_table(key, 202, (EXPERTS * PIECES, D, HID))


def draw_w_down(key, part):
    return integer_table(key, 303, (EXPERTS * PIECES, HID, D))


def levels(own_key, shape, split, smallest, largest):
    level = 1.0
    for axis_at, blocks in split:
        draws = jax.random.uniform(jax.random.fold_in(jax.random.fold_in(own_key, 6), axis_at), (blocks,), jnp.float32, smallest / len(split), largest / len(split))
        level = level * jnp.repeat(jnp.exp(draws), shape[axis_at] // blocks).reshape((-1,) + (1,) * (len(shape) - 1 - axis_at))
    return level


def shared_out(stream_key, own, number, rows, amount, top, limit, skew):
    sequence = jax.random.permutation(stream_key, amount)
    heavy_load, common = load_shares(amount, rows * top, limit, skew, True), load_shares(amount, rows * top, limit, skew, False)
    places = jnp.arange(amount)

    def named(tallies, turn):
        used = int((tallies > 0).sum())
        fixed = max(1, used // 4)
        moved = fixed + (places - fixed + turn * (used - fixed)) % max(1, amount - fixed)
        return jnp.zeros((amount,), jnp.int32).at[sequence[jnp.where(places < fixed, places, moved)]].set(jnp.asarray(tallies, jnp.int32))

    tallies = jnp.where(number % 4 == 0, named(heavy_load, number // 4), named(common, number - number // 4 - 1))
    mixed = jax.random.permutation(jax.random.fold_in(own, 3), amount)
    source_of, taker = mixed[0:amount // 2 * 2:2], mixed[1:amount // 2 * 2:2]
    slack = jnp.minimum(tallies[source_of] - 1, limit - tallies[taker]) // 2
    slack = jnp.where((source_of == sequence[0]) | (taker == sequence[0]) | (tallies[taker] == 0), 0, jnp.maximum(slack, 0))
    moved = jax.random.randint(jax.random.fold_in(own, 4), (amount // 2,), 0, 1 << 20) % (slack + 1)
    tallies = tallies.at[source_of].add(-moved).at[taker].add(moved)
    items = jnp.searchsorted(jnp.cumsum(tallies), jnp.arange(rows * top), side="right").astype(jnp.int32)
    grid = items.reshape(top, rows).T
    grid = grid[jax.random.permutation(jax.random.fold_in(own, 1), rows)]
    turn = jax.random.randint(jax.random.fold_in(own, 2), (rows, 1), 0, top)
    return jnp.take_along_axis(grid, (jnp.arange(top)[None, :] + turn) % top, axis=1)


def load_shares(amount, total, most, skew, full):
    loads = [(1 << 20) // math.isqrt(standing ** skew) + 1 for standing in range(1, amount + 1)]
    largest = most if full else min(most, max(-(-total // amount), total * loads[0] // sum(loads)))
    least = 1 if total - largest >= amount - 1 else 0
    holding, surplus = [largest] + [least] * (amount - 1), total - largest - least * (amount - 1)
    while surplus > 0:
        free = [i for i in range(1, amount) if holding[i] < largest] or [i for i in range(1, amount) if holding[i] < most]
        whole, remaining = sum([loads[i] for i in free]), surplus
        for i in free:
            more = min(most - holding[i], max(1, remaining * loads[i] // whole), surplus)
            holding[i] = holding[i] + more
            surplus = surplus - more
    return np.array(holding)


def bell_draw(own_key, extent, scale, bound, cuts=(), held_as=jnp.bfloat16):
    values = jax.random.normal(own_key, extent, jnp.float32) * scale
    if len(cuts) > 0:
        values = levels(own_key, extent, cuts, -0.22, 0.18) * values
    return jnp.clip(values, min=-bound, max=bound).astype(held_as)


def setup_inputs(seed: int = 0, part: int = 0) -> dict:
    keys = jax.random.split(jax.random.key(seed), 11)
    part_keys = jax.random.split(jax.random.fold_in(keys[10], part), 11)
    act = bell_draw(part_keys[0], (TOKENS, D), 1.0, 6.0, ((0, 16),))
    act_scale = jnp.clip(jnp.exp(math.log(3.0) - 2.306499 * jax.random.uniform(part_keys[1], (TOKENS,), jnp.float32) ** levels(part_keys[1], (TOKENS,), ((0, 16),), -0.2, 0.2)), 0.29882812, 3.0).astype(jnp.bfloat16)
    route_ids_keys = jax.random.split(jax.random.fold_in(part_keys[2], 1), TOKENS // TOK_DEV)
    route_ids_turns = jax.random.permutation(jax.random.fold_in(part_keys[2], 3), TOKENS // TOK_DEV)
    route_ids = jax.vmap(lambda own, number: shared_out(jax.random.fold_in(part_keys[2], 2), own, number, TOK_DEV, EXPERTS, TOP, CAP, 2))(route_ids_keys, route_ids_turns).reshape((TOKENS, TOP))
    route_weights = jnp.clip(0.2 + 0.8 * jax.random.uniform(part_keys[3], (TOKENS, TOP), jnp.float32) ** levels(part_keys[3], (TOKENS, TOP), ((0, 16),), -0.2, 0.2), 0.2, 1.0)
    w_gate = draw_w_gate(jax.random.fold_in(keys[10], 71), part)
    w_up = draw_w_up(jax.random.fold_in(keys[10], 71), part)
    w_down = draw_w_down(jax.random.fold_in(keys[10], 71), part)
    gate_scale = jnp.clip(jnp.exp(math.log(0.00032) - 1.3862944 * jax.random.uniform(keys[7], (EXPERTS * PIECES, HID), jnp.float32) ** levels(keys[7], (EXPERTS * PIECES, HID), ((0, 16),), -0.2, 0.2)), 7.999999797903001e-05, 0.00032)
    up_scale = jnp.clip(jnp.exp(math.log(0.00032) - 1.3862944 * jax.random.uniform(keys[8], (EXPERTS * PIECES, HID), jnp.float32) ** levels(keys[8], (EXPERTS * PIECES, HID), ((0, 16),), -0.2, 0.2)), 7.999999797903001e-05, 0.00032)
    down_scale = jnp.clip(jnp.exp(jax.random.uniform(keys[9], (EXPERTS, D), jnp.float32, math.log(0.0004), math.log(0.0016))), 0.0004, 0.0016)
    return dict(act=act, act_scale=act_scale, route_ids=route_ids, route_weights=route_weights, w_gate=w_gate, w_up=w_up, w_down=w_down, gate_scale=gate_scale, up_scale=up_scale, down_scale=down_scale)


def reference(act, act_scale, route_ids, route_weights, w_gate, w_up, w_down, gate_scale, up_scale, down_scale):
    tokens = act.shape[0]
    rows_max = N_EXPERT * CAP

    def per_expert(expert, total):
        hit = route_ids == expert
        marked = jnp.any(hit, axis=1)
        index = jnp.nonzero(marked, size=rows_max, fill_value=0)[0].astype(jnp.int32)
        valid = (jnp.arange(rows_max) < jnp.sum(marked.astype(jnp.int32))).astype(jnp.float32)
        rows = act[index]
        scales = act_scale[index].astype(jnp.float32)[:, None]
        weight = jnp.sum(jnp.where(hit, route_weights, jnp.zeros_like(route_weights)), axis=1)[index] * valid
        down_row = lax.dynamic_index_in_dim(down_scale, expert, 0, keepdims=False)
        summed = jnp.zeros((rows_max, D), jnp.float32)
        for piece in range(PIECES):
            slot = expert * PIECES + piece
            wg = lax.dynamic_index_in_dim(w_gate, slot, 0, keepdims=False)
            wu = lax.dynamic_index_in_dim(w_up, slot, 0, keepdims=False)
            wd = lax.dynamic_index_in_dim(w_down, slot, 0, keepdims=False)
            gscale = lax.dynamic_index_in_dim(gate_scale, slot, 0, keepdims=False)
            uscale = lax.dynamic_index_in_dim(up_scale, slot, 0, keepdims=False)
            gate = jnp.dot(rows, wg, preferred_element_type=jnp.float32) * scales * gscale[None, :]
            upper = jnp.dot(rows, wu, preferred_element_type=jnp.float32) * scales * uscale[None, :]
            hidden = (jax.nn.silu(gate) * upper).astype(jnp.bfloat16)
            partial_value = (jnp.dot(hidden, wd, preferred_element_type=jnp.float32) * down_row[None, :]).astype(jnp.bfloat16)
            summed = summed + partial_value.astype(jnp.float32)
        expert_out = summed.astype(jnp.bfloat16)
        return total.at[index].add(weight[:, None] * expert_out.astype(jnp.float32))

    total = lax.fori_loop(0, EXPERTS, per_expert, jnp.zeros((tokens, D), jnp.float32))
    return total.astype(jnp.bfloat16)
```

```python
import jax
import jax.numpy as jnp
from jax import lax
from jax.sharding import PartitionSpec as P

PIECES = 2


def body(
    act, act_scale, route_ids, route_weights, w_gate, w_up, w_down, gate_scale, up_scale, down_scale
):
    owner = lax.axis_index("expert") // PIECES
    down_row = lax.dynamic_index_in_dim(down_scale, owner, 0, keepdims=False)
    rows = lax.all_gather(act, "expert", axis=0, tiled=True)
    scales = lax.all_gather(act_scale, "expert", axis=0, tiled=True)
    ids = lax.all_gather(route_ids, "expert", axis=0, tiled=True)
    weights = lax.all_gather(route_weights, "expert", axis=0, tiled=True)
    hit = ids == owner
    weight = jnp.sum(jnp.where(hit, weights, 0.0), axis=1)
    factor = scales[:, None].astype(jnp.float32)
    gate = jnp.dot(rows, w_gate[0], preferred_element_type=jnp.float32) * factor * gate_scale[0][None, :]
    upper = jnp.dot(rows, w_up[0], preferred_element_type=jnp.float32) * factor * up_scale[0][None, :]
    hidden = (jax.nn.silu(gate) * upper).astype(jnp.bfloat16)
    part = jnp.dot(hidden, w_down[0], preferred_element_type=jnp.float32) * down_row[None, :]
    part = (part * weight[:, None]).astype(jnp.bfloat16)
    return lax.psum_scatter(part, "expert", scatter_dimension=0, tiled=True)


def solution(mesh):
    return jax.shard_map(
        body,
        mesh=mesh,
        in_specs=(
            P(("groups", "expert"), None),
            P(("groups", "expert")),
            P(("groups", "expert"), None),
            P(("groups", "expert"), None),
            P("expert", None, None),
            P("expert", None, None),
            P("expert", None, None),
            P("expert", None),
            P("expert", None),
            P(),
        ),
        out_specs=P(("groups", "expert"), None),
        check_vma=False,
    )
```

```python
import functools
import math

import jax
import jax.numpy as jnp
from jax import lax
from jax.experimental import pallas as pl
from jax.experimental.pallas import tpu as pltpu
from jax.sharding import PartitionSpec as P

PIECES = 2
X_SLOTS = 4
ACC_SLOTS = 3


def kernel(
    n, snake, experts, x_hbm, wg_hbm, wu_hbm, wd_hbm, gs_ref, us_ref, down_ref, out_ref,
    xb, acc_in, acc_out, sp_in, sp_out, wg, wu, wd, hid,
    load_sem, x_send, x_recv, a_send, a_recv, sx_sem, sp_sem,
):
    rows, width = out_ref.shape
    half = rows // 2
    hidden = hid.shape[1]
    me = lax.axis_index("expert")
    core = me % 2
    chip = me // 2
    sib = chip * 2 + (1 - core)
    if snake:
        odd = chip % 2
        pos = (1 - odd) * (chip // 2) + odd * (n - 1 - chip // 2)
    else:
        pos = chip

    def device_at(p):
        p = p % n
        if snake:
            high = p // (n // 2)
            p = (1 - high) * (2 * p) + high * (2 * (n - 1 - p) + 1)
        return p * 2 + core

    ahead = device_at(pos + 1)
    behind = device_at(pos + n - 1)

    def remote(src, dst, send, recv, target):
        return pltpu.make_async_remote_copy(
            src_ref=src, dst_ref=dst, send_sem=send, recv_sem=recv,
            device_id={"expert": target}, device_id_type=pl.DeviceIdType.MESH,
        )

    def ring_x(s):
        a, b = s % X_SLOTS, (s + 1) % X_SLOTS
        return [
            remote(xb.at[a, pl.ds(d * half, half)], xb.at[b, pl.ds(d * half, half)],
                   x_send.at[d, a], x_recv.at[d, b], to)
            for d, to in enumerate((ahead, behind))
        ]

    def ring_acc(s):
        a, b = s % 2, (s + 1) % ACC_SLOTS
        return [
            remote(acc_out.at[a, pl.ds(d * half, half)], acc_in.at[b, pl.ds(d * half, half)],
                   a_send.at[d, a], a_recv.at[d, b], to)
            for d, to in enumerate((ahead, behind))
        ]

    def sib_x(s):
        a = s % X_SLOTS
        return remote(xb.at[a, pl.ds(0, rows)], xb.at[a, pl.ds(rows, rows)],
                      sx_sem.at[0, a], sx_sem.at[1, a], sib)

    def sib_part(s):
        a = s % 2
        return remote(sp_out.at[a], sp_in.at[a], sp_sem.at[0, a], sp_sem.at[1, a], sib)

    first = pltpu.make_async_copy(x_hbm, xb.at[0, pl.ds(0, rows)], load_sem.at[0])
    first.start()
    loads = [
        pltpu.make_async_copy(src, dst, load_sem.at[1 + i])
        for i, (src, dst) in enumerate(((wg_hbm, wg), (wu_hbm, wu), (wd_hbm, wd)))
    ]
    for load in loads:
        load.start()
    barrier = pltpu.get_barrier_semaphore()
    for other in (ahead, behind, sib):
        pl.semaphore_signal(barrier, inc=1, device_id={"expert": other},
                            device_id_type=pl.DeviceIdType.MESH)
    pl.semaphore_wait(barrier, 3)
    first.wait()

    tile = math.gcd(width, 512)
    htile = math.gcd(hidden, 256)

    def step(s, carry):
        slot = s % X_SLOTS
        out_slot = s % 2

        @pl.when(s >= 1)
        def _():
            for copy in ring_x(s - 1):
                copy.wait_recv()

        @pl.when(s >= 2)
        def _():
            for copy in ring_x(s - 2):
                copy.wait_send()

        @pl.when(s < n - 1)
        def _():
            for copy in ring_x(s):
                copy.start()

        to_sib = sib_x(s)
        to_sib.start()
        to_sib.wait()

        @pl.when(s == 0)
        def _():
            for load in loads:
                load.wait()

        @pl.when(s >= 3)
        def _():
            for copy in ring_acc(s - 2):
                copy.wait_send()

        meta = xb[slot, :, width:].astype(jnp.float32)
        lane = lax.broadcasted_iota(jnp.int32, meta.shape, 1)
        mine = (lane == chip) | (lane == experts + chip)
        weight = jnp.sum(jnp.where(mine, meta, 0.0), axis=1, keepdims=True)
        factor = jnp.sum(jnp.where(lane == 2 * experts, meta, 0.0), axis=1, keepdims=True)

        @pl.loop(0, hidden // htile)
        def _(j):
            cols = pl.ds(pl.multiple_of(j * htile, htile), htile)
            rows_x = xb[slot, :, :width]
            gate = jnp.dot(rows_x, wg[:, cols], preferred_element_type=jnp.float32)
            gate = gate * factor * gs_ref[:, cols]
            upper = jnp.dot(rows_x, wu[:, cols], preferred_element_type=jnp.float32)
            upper = upper * factor * us_ref[:, cols]
            hid[:, cols] = (gate / (1.0 + jnp.exp(-gate)) * upper).astype(jnp.bfloat16)

        @pl.loop(0, width // tile)
        def _(t):
            cols = pl.ds(pl.multiple_of(t * tile, tile), tile)
            part = jnp.dot(hid[...], wd[:, cols], preferred_element_type=jnp.float32)
            part = (part * down_ref[:, cols] * weight).astype(jnp.bfloat16)
            acc_out[out_slot, :, cols] = part[:rows]
            sp_out[out_slot, :, cols] = part[rows:]

        exchange = sib_part(s)
        exchange.start()
        exchange.wait()

        def both(cols):
            return acc_out[out_slot, :, cols].astype(jnp.float32) + sp_in[
                out_slot, :, cols
            ].astype(jnp.float32)

        @pl.when(s == 0)
        def _():
            @pl.loop(0, width // tile)
            def _(t):
                cols = pl.ds(pl.multiple_of(t * tile, tile), tile)
                out_ref[:, cols] = both(cols).astype(jnp.bfloat16)

        @pl.when(s == 1)
        def _():
            @pl.loop(0, width // tile)
            def _(t):
                cols = pl.ds(pl.multiple_of(t * tile, tile), tile)
                acc_out[out_slot, :, cols] = both(cols).astype(jnp.bfloat16)

        @pl.when(s >= 2)
        def _():
            for copy in ring_acc(s - 1):
                copy.wait_recv()
            in_slot = s % ACC_SLOTS

            @pl.loop(0, width // tile)
            def _(t):
                cols = pl.ds(pl.multiple_of(t * tile, tile), tile)
                total = both(cols) + acc_in[in_slot, :, cols].astype(jnp.float32)
                acc_out[out_slot, :, cols] = total.astype(jnp.bfloat16)

        @pl.when(s >= 1)
        def _():
            for copy in ring_acc(s):
                copy.start()

        return carry

    lax.fori_loop(0, n, step, 0)
    for copy in ring_acc(n - 1):
        copy.wait_recv()

    @pl.loop(0, width // tile)
    def _(t):
        cols = pl.ds(pl.multiple_of(t * tile, tile), tile)
        total = out_ref[:, cols].astype(jnp.float32) + acc_in[n % ACC_SLOTS, :, cols].astype(
            jnp.float32
        )
        out_ref[:, cols] = total.astype(jnp.bfloat16)

    for copy in ring_x(n - 2) + ring_acc(n - 2) + ring_acc(n - 1):
        copy.wait_send()


def body(
    snake, act, act_scale, route_ids, route_weights, w_gate, w_up, w_down, gate_scale, up_scale,
    down_scale
):
    rows, width = act.shape
    experts = down_scale.shape[0]
    hidden = w_gate.shape[2]
    n = lax.axis_size("expert") // PIECES
    owner = lax.axis_index("expert") // PIECES
    down_row = lax.dynamic_slice_in_dim(down_scale, owner, 1, 0)
    hit = route_ids[:, :, None] == jnp.arange(experts, dtype=jnp.int32)[None, None, :]
    dense = jnp.sum(jnp.where(hit, route_weights[:, :, None], 0.0), axis=1)
    high = lax.reduce_precision(dense, 8, 7)
    low = dense - high
    used = 2 * experts + 1
    extra = -(-used // 128) * 128
    meta = jnp.concatenate(
        [high.astype(jnp.bfloat16), low.astype(jnp.bfloat16), act_scale[:, None],
         jnp.zeros((rows, extra - used), jnp.bfloat16)], axis=1)
    x = jnp.concatenate([act, meta], axis=1)
    bf16 = jnp.bfloat16
    anywhere = pl.BlockSpec(memory_space=pl.ANY)
    vmem = pl.BlockSpec(memory_space=pltpu.VMEM)
    dma = pltpu.SemaphoreType.DMA
    return pl.pallas_call(
        functools.partial(kernel, n, snake, experts),
        out_shape=jax.ShapeDtypeStruct((rows, width), bf16),
        in_specs=[anywhere] * 4 + [vmem] * 3,
        out_specs=vmem,
        scratch_shapes=[
            pltpu.VMEM((X_SLOTS, 2 * rows, width + extra), bf16),
            pltpu.VMEM((ACC_SLOTS, rows, width), bf16),
            pltpu.VMEM((2, rows, width), bf16),
            pltpu.VMEM((2, rows, width), bf16),
            pltpu.VMEM((2, rows, width), bf16),
            pltpu.VMEM((width, hidden), bf16),
            pltpu.VMEM((width, hidden), bf16),
            pltpu.VMEM((hidden, width), bf16),
            pltpu.VMEM((2 * rows, hidden), bf16),
            dma((4,)), dma((2, X_SLOTS)), dma((2, X_SLOTS)),
            dma((2, 2)), dma((2, ACC_SLOTS)), dma((2, X_SLOTS)), dma((2, 2)),
        ],
        compiler_params=pltpu.CompilerParams(
            collective_id=0, has_side_effects=True, vmem_limit_bytes=62 * 1024 * 1024
        ),
    )(x, w_gate[0], w_up[0], w_down[0], gate_scale, up_scale, down_row)


def winds_back(mesh):
    chips = [getattr(d, "coords", None) for d in mesh.devices[0][::PIECES]]
    if any(c is None for c in chips):
        return False
    return sum(len({c[i] for c in chips}) > 1 for i in range(len(chips[0]))) == 2


def solution(mesh):
    return jax.shard_map(
        functools.partial(body, winds_back(mesh)),
        mesh=mesh,
        in_specs=(
            P(("groups", "expert"), None),
            P(("groups", "expert")),
            P(("groups", "expert"), None),
            P(("groups", "expert"), None),
            P("expert", None, None),
            P("expert", None, None),
            P("expert", None, None),
            P("expert", None),
            P("expert", None),
            P(),
        ),
        out_specs=P(("groups", "expert"), None),
        check_vma=False,
    )
```

```python
import functools
import math

import jax
import jax.numpy as jnp
from jax import lax
from jax.experimental import pallas as pl
from jax.experimental.pallas import tpu as pltpu
from jax.sharding import PartitionSpec as P

PIECES = 2
X_SLOTS = 4
ACC_SLOTS = 3
BANDS = 2


def kernel(
    n, snake, experts, x_hbm, meta_hbm, wg_hbm, wu_hbm, wd_hbm, gs_ref, us_ref, down_ref, out_ref,
    xb, acc_in, acc_out, sp_in, sp_out, wg, wu, wd, hid,
    load_sem, x_send, x_recv, a_send, a_recv, sx_sem, sp_sem,
):
    rows, width = out_ref.shape
    half = rows // 2
    hidden = hid.shape[1]
    me = lax.axis_index("expert")
    core = me % 2
    chip = me // 2
    sib = chip * 2 + (1 - core)
    if snake:
        odd = chip % 2
        pos = (1 - odd) * (chip // 2) + odd * (n - 1 - chip // 2)
    else:
        pos = chip

    def device_at(p):
        p = p % n
        if snake:
            high = p // (n // 2)
            p = (1 - high) * (2 * p) + high * (2 * (n - 1 - p) + 1)
        return p * 2 + core

    ahead = device_at(pos + 1)
    behind = device_at(pos + n - 1)

    def remote(src, dst, send, recv, target):
        return pltpu.make_async_remote_copy(
            src_ref=src, dst_ref=dst, send_sem=send, recv_sem=recv,
            device_id={"expert": target}, device_id_type=pl.DeviceIdType.MESH,
        )

    def ring_x(s):
        a, b = s % X_SLOTS, (s + 1) % X_SLOTS
        return [
            remote(xb.at[a, pl.ds(d * half, half)], xb.at[b, pl.ds(d * half, half)],
                   x_send.at[d, a], x_recv.at[d, b], to)
            for d, to in enumerate((ahead, behind))
        ]

    band = width // BANDS

    def ring_acc(s, k):
        a, b = s % 2, (s + 1) % ACC_SLOTS
        cols = pl.ds(k * band, band)
        return [
            remote(acc_out.at[a, pl.ds(d * half, half), cols],
                   acc_in.at[b, pl.ds(d * half, half), cols],
                   a_send.at[d, k, a], a_recv.at[d, k, b], to)
            for d, to in enumerate((ahead, behind))
        ]

    def sib_x(s):
        a = s % X_SLOTS
        return remote(xb.at[a, pl.ds(0, rows)], xb.at[a, pl.ds(rows, rows)],
                      sx_sem.at[0, a], sx_sem.at[1, a], sib)

    def sib_part(s):
        a = s % 2
        return remote(sp_out.at[a], sp_in.at[a], sp_sem.at[0, a], sp_sem.at[1, a], sib)

    first = [
        pltpu.make_async_copy(x_hbm, xb.at[0, pl.ds(0, rows), pl.ds(0, width)], load_sem.at[3]),
        pltpu.make_async_copy(
            meta_hbm, xb.at[0, pl.ds(0, rows), pl.ds(width, meta_hbm.shape[1])], load_sem.at[4]
        ),
    ]
    for load in first:
        load.start()
    loads = [
        pltpu.make_async_copy(src, dst, load_sem.at[i])
        for i, (src, dst) in enumerate(((wg_hbm, wg), (wu_hbm, wu), (wd_hbm, wd)))
    ]
    for load in loads:
        load.start()
    barrier = pltpu.get_barrier_semaphore()
    for other in (ahead, behind, sib):
        pl.semaphore_signal(barrier, inc=1, device_id={"expert": other},
                            device_id_type=pl.DeviceIdType.MESH)
    pl.semaphore_wait(barrier, 3)
    for load in first:
        load.wait()
    for copy in ring_x(0):
        copy.start()
    sib_x(0).start()

    tile = math.gcd(band, 512)
    htile = math.gcd(hidden, 256)

    def step(s, carry):
        slot = s % X_SLOTS
        out_slot = s % 2

        sib_x(s).wait()

        @pl.when(s == 0)
        def _():
            for load in loads:
                load.wait()

        @pl.when(s >= 3)
        def _():
            for k in range(BANDS):
                for copy in ring_acc(s - 2, k):
                    copy.wait_send()

        meta = xb[slot, :, width:].astype(jnp.float32)
        lane = lax.broadcasted_iota(jnp.int32, meta.shape, 1)
        mine = (lane == chip) | (lane == experts + chip)
        weight = jnp.sum(jnp.where(mine, meta, 0.0), axis=1, keepdims=True)
        factor = jnp.sum(jnp.where(lane == 2 * experts, meta, 0.0), axis=1, keepdims=True)

        @pl.loop(0, hidden // htile)
        def _(j):
            cols = pl.ds(pl.multiple_of(j * htile, htile), htile)
            rows_x = xb[slot, :, :width]
            gate = jnp.dot(rows_x, wg[:, cols], preferred_element_type=jnp.float32)
            gate = gate * factor * gs_ref[:, cols]
            upper = jnp.dot(rows_x, wu[:, cols], preferred_element_type=jnp.float32)
            upper = upper * factor * us_ref[:, cols]
            hid[:, cols] = (gate / (1.0 + jnp.exp(-gate)) * upper).astype(jnp.bfloat16)

        @pl.when(s < n - 1)
        def _():
            for copy in ring_x(s):
                copy.wait_recv()

            @pl.when(s >= 1)
            def _():
                for copy in ring_x(s - 1):
                    copy.wait_send()

            @pl.when(s < n - 2)
            def _():
                for copy in ring_x(s + 1):
                    copy.start()

            sib_x(s + 1).start()

        @pl.loop(0, width // tile)
        def _(t):
            cols = pl.ds(pl.multiple_of(t * tile, tile), tile)
            part = jnp.dot(hid[...], wd[:, cols], preferred_element_type=jnp.float32)
            part = (part * down_ref[:, cols] * weight).astype(jnp.bfloat16)
            acc_out[out_slot, :, cols] = part[:rows]
            sp_out[out_slot, :, cols] = part[rows:]

        exchange = sib_part(s)
        exchange.start()
        exchange.wait()

        def both(cols):
            return acc_out[out_slot, :, cols].astype(jnp.float32) + sp_in[
                out_slot, :, cols
            ].astype(jnp.float32)

        @pl.when(s == 0)
        def _():
            @pl.loop(0, width // tile)
            def _(t):
                cols = pl.ds(pl.multiple_of(t * tile, tile), tile)
                out_ref[:, cols] = both(cols).astype(jnp.bfloat16)

        for k in range(BANDS):
            @pl.when(s == 1)
            def _():
                @pl.loop(0, band // tile)
                def _(t):
                    cols = pl.ds(pl.multiple_of(k * band + t * tile, tile), tile)
                    acc_out[out_slot, :, cols] = both(cols).astype(jnp.bfloat16)

            @pl.when(s >= 2)
            def _():
                for copy in ring_acc(s - 1, k):
                    copy.wait_recv()
                in_slot = s % ACC_SLOTS

                @pl.loop(0, band // tile)
                def _(t):
                    cols = pl.ds(pl.multiple_of(k * band + t * tile, tile), tile)
                    total = both(cols) + acc_in[in_slot, :, cols].astype(jnp.float32)
                    acc_out[out_slot, :, cols] = total.astype(jnp.bfloat16)

            @pl.when(s >= 1)
            def _():
                for copy in ring_acc(s, k):
                    copy.start()

        return carry

    lax.fori_loop(0, n, step, 0)
    for k in range(BANDS):
        for copy in ring_acc(n - 1, k):
            copy.wait_recv()

        @pl.loop(0, band // tile)
        def _(t):
            cols = pl.ds(pl.multiple_of(k * band + t * tile, tile), tile)
            total = out_ref[:, cols].astype(jnp.float32) + acc_in[n % ACC_SLOTS, :, cols].astype(
                jnp.float32
            )
            out_ref[:, cols] = total.astype(jnp.bfloat16)

    for copy in ring_x(n - 2):
        copy.wait_send()
    for k in range(BANDS):
        for copy in ring_acc(n - 2, k) + ring_acc(n - 1, k):
            copy.wait_send()


def body(
    snake, act, act_scale, route_ids, route_weights, w_gate, w_up, w_down, gate_scale, up_scale,
    down_scale
):
    rows, width = act.shape
    experts = down_scale.shape[0]
    hidden = w_gate.shape[2]
    n = lax.axis_size("expert") // PIECES
    owner = lax.axis_index("expert") // PIECES
    down_row = lax.dynamic_slice_in_dim(down_scale, owner, 1, 0)
    hit = route_ids[:, :, None] == jnp.arange(experts, dtype=jnp.int32)[None, None, :]
    dense = jnp.sum(jnp.where(hit, route_weights[:, :, None], 0.0), axis=1)
    high = lax.reduce_precision(dense, 8, 7)
    low = dense - high
    used = 2 * experts + 1
    extra = -(-used // 128) * 128
    meta = jnp.concatenate(
        [high.astype(jnp.bfloat16), low.astype(jnp.bfloat16), act_scale[:, None],
         jnp.zeros((rows, extra - used), jnp.bfloat16)], axis=1)
    bf16 = jnp.bfloat16
    anywhere = pl.BlockSpec(memory_space=pl.ANY)
    vmem = pl.BlockSpec(memory_space=pltpu.VMEM)
    dma = pltpu.SemaphoreType.DMA
    return pl.pallas_call(
        functools.partial(kernel, n, snake, experts),
        out_shape=jax.ShapeDtypeStruct((rows, width), bf16),
        in_specs=[anywhere] * 5 + [vmem] * 3,
        out_specs=vmem,
        scratch_shapes=[
            pltpu.VMEM((X_SLOTS, 2 * rows, width + extra), bf16),
            pltpu.VMEM((ACC_SLOTS, rows, width), bf16),
            pltpu.VMEM((2, rows, width), bf16),
            pltpu.VMEM((2, rows, width), bf16),
            pltpu.VMEM((2, rows, width), bf16),
            pltpu.VMEM((width, hidden), bf16),
            pltpu.VMEM((width, hidden), bf16),
            pltpu.VMEM((hidden, width), bf16),
            pltpu.VMEM((2 * rows, hidden), bf16),
            dma((5,)), dma((2, X_SLOTS)), dma((2, X_SLOTS)),
            dma((2, BANDS, 2)), dma((2, BANDS, ACC_SLOTS)), dma((2, X_SLOTS)), dma((2, 2)),
        ],
        compiler_params=pltpu.CompilerParams(
            collective_id=0, has_side_effects=True, vmem_limit_bytes=62 * 1024 * 1024
        ),
    )(act, meta, w_gate[0], w_up[0], w_down[0], gate_scale, up_scale, down_row)


def winds_back(mesh):
    chips = [getattr(d, "coords", None) for d in mesh.devices[0][::PIECES]]
    if any(c is None for c in chips):
        return False
    return sum(len({c[i] for c in chips}) > 1 for i in range(len(chips[0]))) == 2


def solution(mesh):
    return jax.shard_map(
        functools.partial(body, winds_back(mesh)),
        mesh=mesh,
        in_specs=(
            P(("groups", "expert"), None),
            P(("groups", "expert")),
            P(("groups", "expert"), None),
            P(("groups", "expert"), None),
            P("expert", None, None),
            P("expert", None, None),
            P("expert", None, None),
            P("expert", None),
            P("expert", None),
            P(),
        ),
        out_specs=P(("groups", "expert"), None),
        check_vma=False,
    )
```

```python
import functools
import math

import jax
import jax.numpy as jnp
from jax import lax
from jax.experimental import pallas as pl
from jax.experimental.pallas import tpu as pltpu
from jax.sharding import PartitionSpec as P

PIECES = 2
X_SLOTS = 4
ACC_SLOTS = 3
BANDS = 4


def kernel(
    n, snake, experts, x_hbm, meta_hbm, wg_hbm, wu_hbm, wd_hbm, gs_ref, us_ref, down_ref, out_ref,
    xb, acc_in, acc_out, sp_in, sp_out, wg, wu, wd, hid,
    load_sem, x_send, x_recv, a_send, a_recv, sx_sem, sp_sem,
):
    rows, width = out_ref.shape
    half = rows // 2
    hidden = hid.shape[1]
    me = lax.axis_index("expert")
    core = me % 2
    chip = me // 2
    sib = chip * 2 + (1 - core)
    if snake:
        odd = chip % 2
        pos = (1 - odd) * (chip // 2) + odd * (n - 1 - chip // 2)
    else:
        pos = chip

    def device_at(p):
        p = p % n
        if snake:
            high = p // (n // 2)
            p = (1 - high) * (2 * p) + high * (2 * (n - 1 - p) + 1)
        return p * 2 + core

    ahead = device_at(pos + 1)
    behind = device_at(pos + n - 1)

    def remote(src, dst, send, recv, target):
        return pltpu.make_async_remote_copy(
            src_ref=src, dst_ref=dst, send_sem=send, recv_sem=recv,
            device_id={"expert": target}, device_id_type=pl.DeviceIdType.MESH,
        )

    def ring_x(s):
        a, b = s % X_SLOTS, (s + 1) % X_SLOTS
        return [
            remote(xb.at[a, pl.ds(d * half, half)], xb.at[b, pl.ds(d * half, half)],
                   x_send.at[d, a], x_recv.at[d, b], to)
            for d, to in enumerate((ahead, behind))
        ]

    band = width // BANDS

    def ring_acc(s, k):
        a, b = s % 2, (s + 1) % ACC_SLOTS
        cols = pl.ds(k * band, band)
        return [
            remote(acc_out.at[a, pl.ds(d * half, half), cols],
                   acc_in.at[b, pl.ds(d * half, half), cols],
                   a_send.at[d, k, a], a_recv.at[d, k, b], to)
            for d, to in enumerate((ahead, behind))
        ]

    def sib_x(s):
        a = s % X_SLOTS
        return remote(xb.at[a, pl.ds(0, rows)], xb.at[a, pl.ds(rows, rows)],
                      sx_sem.at[0, a], sx_sem.at[1, a], sib)

    def sib_part(s, k):
        a = s % 2
        cols = pl.ds(k * band, band)
        return remote(sp_out.at[a, :, cols], sp_in.at[a, :, cols],
                      sp_sem.at[0, k, a], sp_sem.at[1, k, a], sib)

    first = [
        pltpu.make_async_copy(x_hbm, xb.at[0, pl.ds(0, rows), pl.ds(0, width)], load_sem.at[3]),
        pltpu.make_async_copy(
            meta_hbm, xb.at[0, pl.ds(0, rows), pl.ds(width, meta_hbm.shape[1])], load_sem.at[4]
        ),
    ]
    for load in first:
        load.start()
    loads = [
        pltpu.make_async_copy(src, dst, load_sem.at[i])
        for i, (src, dst) in enumerate(((wg_hbm, wg), (wu_hbm, wu), (wd_hbm, wd)))
    ]
    for load in loads:
        load.start()
    barrier = pltpu.get_barrier_semaphore()
    for other in (ahead, behind, sib):
        pl.semaphore_signal(barrier, inc=1, device_id={"expert": other},
                            device_id_type=pl.DeviceIdType.MESH)
    pl.semaphore_wait(barrier, 3)
    for load in first:
        load.wait()
    for copy in ring_x(0):
        copy.start()
    sib_x(0).start()

    tile = band if band % 256 == 0 else math.gcd(band, 256)
    htile = math.gcd(hidden, 256)

    def step(s, carry):
        slot = s % X_SLOTS
        out_slot = s % 2

        sib_x(s).wait()

        @pl.when(s == 0)
        def _():
            for load in loads:
                load.wait()

        @pl.when(s >= 3)
        def _():
            for k in range(BANDS):
                for copy in ring_acc(s - 2, k):
                    copy.wait_send()

        meta = xb[slot, :, width:].astype(jnp.float32)
        lane = lax.broadcasted_iota(jnp.int32, meta.shape, 1)
        mine = (lane == chip) | (lane == experts + chip)
        weight = jnp.sum(jnp.where(mine, meta, 0.0), axis=1, keepdims=True)
        factor = jnp.sum(jnp.where(lane == 2 * experts, meta, 0.0), axis=1, keepdims=True)

        @pl.loop(0, hidden // htile)
        def _(j):
            cols = pl.ds(pl.multiple_of(j * htile, htile), htile)
            rows_x = xb[slot, :, :width]
            gate = jnp.dot(rows_x, wg[:, cols], preferred_element_type=jnp.float32)
            gate = gate * factor * gs_ref[:, cols]
            upper = jnp.dot(rows_x, wu[:, cols], preferred_element_type=jnp.float32)
            upper = upper * factor * us_ref[:, cols]
            hid[:, cols] = (gate / (1.0 + jnp.exp(-gate)) * upper).astype(jnp.bfloat16)

        @pl.when(s < n - 1)
        def _():
            for copy in ring_x(s):
                copy.wait_recv()

            @pl.when(s >= 1)
            def _():
                for copy in ring_x(s - 1):
                    copy.wait_send()

            @pl.when(s < n - 2)
            def _():
                for copy in ring_x(s + 1):
                    copy.start()

            sib_x(s + 1).start()

        for k in range(BANDS):
            @pl.loop(0, band // tile)
            def _(t):
                cols = pl.ds(pl.multiple_of(k * band + t * tile, tile), tile)
                part = jnp.dot(hid[...], wd[:, cols], preferred_element_type=jnp.float32)
                part = (part * down_ref[:, cols] * weight).astype(jnp.bfloat16)
                acc_out[out_slot, :, cols] = part[:rows]
                sp_out[out_slot, :, cols] = part[rows:]

            sib_part(s, k).start()

        def both(cols):
            return acc_out[out_slot, :, cols].astype(jnp.float32) + sp_in[
                out_slot, :, cols
            ].astype(jnp.float32)

        for k in range(BANDS):
            sib_part(s, k).wait()

            @pl.when(s == 0)
            def _():
                @pl.loop(0, band // tile)
                def _(t):
                    cols = pl.ds(pl.multiple_of(k * band + t * tile, tile), tile)
                    out_ref[:, cols] = both(cols).astype(jnp.bfloat16)

            @pl.when(s == 1)
            def _():
                @pl.loop(0, band // tile)
                def _(t):
                    cols = pl.ds(pl.multiple_of(k * band + t * tile, tile), tile)
                    acc_out[out_slot, :, cols] = both(cols).astype(jnp.bfloat16)

            @pl.when(s >= 2)
            def _():
                for copy in ring_acc(s - 1, k):
                    copy.wait_recv()
                in_slot = s % ACC_SLOTS

                @pl.loop(0, band // tile)
                def _(t):
                    cols = pl.ds(pl.multiple_of(k * band + t * tile, tile), tile)
                    total = both(cols) + acc_in[in_slot, :, cols].astype(jnp.float32)
                    acc_out[out_slot, :, cols] = total.astype(jnp.bfloat16)

            @pl.when(s >= 1)
            def _():
                for copy in ring_acc(s, k):
                    copy.start()

        return carry

    lax.fori_loop(0, n, step, 0)
    for k in range(BANDS):
        for copy in ring_acc(n - 1, k):
            copy.wait_recv()

        @pl.loop(0, band // tile)
        def _(t):
            cols = pl.ds(pl.multiple_of(k * band + t * tile, tile), tile)
            total = out_ref[:, cols].astype(jnp.float32) + acc_in[n % ACC_SLOTS, :, cols].astype(
                jnp.float32
            )
            out_ref[:, cols] = total.astype(jnp.bfloat16)

    for copy in ring_x(n - 2):
        copy.wait_send()
    for k in range(BANDS):
        for copy in ring_acc(n - 2, k) + ring_acc(n - 1, k):
            copy.wait_send()


def body(
    snake, act, act_scale, route_ids, route_weights, w_gate, w_up, w_down, gate_scale, up_scale,
    down_scale
):
    rows, width = act.shape
    experts = down_scale.shape[0]
    hidden = w_gate.shape[2]
    n = lax.axis_size("expert") // PIECES
    owner = lax.axis_index("expert") // PIECES
    down_row = lax.dynamic_slice_in_dim(down_scale, owner, 1, 0)
    hit = route_ids[:, :, None] == jnp.arange(experts, dtype=jnp.int32)[None, None, :]
    dense = jnp.sum(jnp.where(hit, route_weights[:, :, None], 0.0), axis=1)
    high = lax.reduce_precision(dense, 8, 7)
    low = dense - high
    used = 2 * experts + 1
    extra = -(-used // 128) * 128
    meta = jnp.concatenate(
        [high.astype(jnp.bfloat16), low.astype(jnp.bfloat16), act_scale[:, None],
         jnp.zeros((rows, extra - used), jnp.bfloat16)], axis=1)
    bf16 = jnp.bfloat16
    anywhere = pl.BlockSpec(memory_space=pl.ANY)
    vmem = pl.BlockSpec(memory_space=pltpu.VMEM)
    dma = pltpu.SemaphoreType.DMA
    return pl.pallas_call(
        functools.partial(kernel, n, snake, experts),
        out_shape=jax.ShapeDtypeStruct((rows, width), bf16),
        in_specs=[anywhere] * 5 + [vmem] * 3,
        out_specs=vmem,
        scratch_shapes=[
            pltpu.VMEM((X_SLOTS, 2 * rows, width + extra), bf16),
            pltpu.VMEM((ACC_SLOTS, rows, width), bf16),
            pltpu.VMEM((2, rows, width), bf16),
            pltpu.VMEM((2, rows, width), bf16),
            pltpu.VMEM((2, rows, width), bf16),
            pltpu.VMEM((width, hidden), bf16),
            pltpu.VMEM((width, hidden), bf16),
            pltpu.VMEM((hidden, width), bf16),
            pltpu.VMEM((2 * rows, hidden), bf16),
            dma((5,)), dma((2, X_SLOTS)), dma((2, X_SLOTS)),
            dma((2, BANDS, 2)), dma((2, BANDS, ACC_SLOTS)), dma((2, X_SLOTS)), dma((2, BANDS, 2)),
        ],
        compiler_params=pltpu.CompilerParams(
            collective_id=0, has_side_effects=True, vmem_limit_bytes=62 * 1024 * 1024
        ),
    )(act, meta, w_gate[0], w_up[0], w_down[0], gate_scale, up_scale, down_row)


def winds_back(mesh):
    chips = [getattr(d, "coords", None) for d in mesh.devices[0][::PIECES]]
    if any(c is None for c in chips):
        return False
    return sum(len({c[i] for c in chips}) > 1 for i in range(len(chips[0]))) == 2


def solution(mesh):
    return jax.shard_map(
        functools.partial(body, winds_back(mesh)),
        mesh=mesh,
        in_specs=(
            P(("groups", "expert"), None),
            P(("groups", "expert")),
            P(("groups", "expert"), None),
            P(("groups", "expert"), None),
            P("expert", None, None),
            P("expert", None, None),
            P("expert", None, None),
            P("expert", None),
            P("expert", None),
            P(),
        ),
        out_specs=P(("groups", "expert"), None),
        check_vma=False,
    )
```
